512 devices in a mesh: dp: 64 (over x_lo, z, core), pipe: 8 (over y, x_hi).
Axes of the slice: x: 4 (x_hi: 2, x_lo: 2; x = x_hi * 2 + x_lo), y: 4, z: 16, core: 2. Of those that a mesh axis runs over, the one named last changes fastest.
Arguments:
- pixels: bfloat16 [4, 2048, 512], P(None, 'dp'), may hold values from -6 to 6
- cotangent: bfloat16 [4, 2048, 512], P(None, 'dp'), may hold values from -6 to 6
- weights_a: bfloat16 [2, 8, 512, 512], P(None, 'pipe'), may hold values from -0.25 to 0.25
- weights_b: bfloat16 [2, 8, 512, 512], P(None, 'pipe'), may hold values from -0.25 to 0.25
Outputs:
- grads_a: float32 [2, 8, 512, 512], P(None, 'pipe', 'dp')
- grads_b: float32 [2, 8, 512, 512], P(None, 'pipe', 'dp')
The draws below stay inside these ranges and needn't reach their ends.
All inputs are finite; a program needn't handle non-finite values.
Results may differ from the reference program's by a relative error of at most 0.023.
Values may be sent and summed in bfloat16 or wider, within the bound.
No kernel may reach another device: no remote copies, remote signals or barrier semaphores. Data moves between devices by JAX's collectives and lax.ppermute only.
A program may use at most 64 MiB of HBM per device.

```python
import math
import jax
import jax.numpy as jnp
from jax import lax

C = 512
M = 4
TOKENS = 2048
N_PIPE = 8


def shard_levels(stream_key, dims, cuts, least, top_value):
    loudness = 1.0
    for position, blocks in cuts:
        heights = jax.random.uniform(jax.random.fold_in(jax.random.fold_in(stream_key, 6), position), (blocks,), jnp.float32, least / len(cuts), top_value / len(cuts))
        loudness = loudness * jnp.repeat(jnp.exp(heights), dims[position] // blocks).reshape((-1,) + (1,) * (len(dims) - 1 - position))
    return loudness


def normal_values(own_key, extent, width, most, shards=(), kind=jnp.bfloat16):
    result = width * jax.random.normal(own_key, extent, jnp.float32)
    if shards:
        result = result * shard_levels(own_key, extent, shards, -0.22, 0.18)
    return jnp.clip(result, -most, most).astype(kind)


def setup_inputs(seed: int = 0) -> dict:
    streams_of = jax.random.split(jax.random.key(seed), 5)
    return {
        "pixels": normal_values(streams_of[0], (M, TOKENS, C), 1.0, 6.0, ((1, 64),)),
        "cotangent": normal_values(streams_of[1], (M, TOKENS, C), 1.0, 6.0, ((1, 64),)),
        "weights_a": normal_values(streams_of[2], (2, N_PIPE, C, C), C ** -0.5, 0.25, ((1, 8),)),
        "weights_b": normal_values(streams_of[3], (2, N_PIPE, C, C), C ** -0.5, 0.25, ((1, 8),)),
    }


EPS = 1e-06

def run_block(section_in, weight_a, weight_b):
    inv_rms = lax.rsqrt(lax.optimization_barrier(jnp.mean(section_in * section_in, axis=-1, keepdims=True)) + EPS)
    normed = section_in * inv_rms
    normed_low = normed.astype(jnp.bfloat16)
    pre_act = jnp.dot(normed_low, weight_a, preferred_element_type=jnp.float32)
    hidden = jax.nn.silu(pre_act).astype(jnp.bfloat16)
    branch = jnp.dot(hidden, weight_b, preferred_element_type=jnp.float32)
    return ((section_in + branch).astype(jnp.bfloat16), (inv_rms, normed, normed_low, pre_act, hidden))

def back_block(grad_out, saved, weight_a, weight_b):
    inv_rms, normed, normed_low, pre_act, hidden = saved
    grad_hidden = jnp.dot(grad_out, weight_b.T, preferred_element_type=jnp.float32)
    grad_b = jnp.dot(hidden.T, grad_out, preferred_element_type=jnp.float32)
    sigmoid_z = jax.nn.sigmoid(pre_act)
    grad_pre = (grad_hidden * sigmoid_z * (1.0 + pre_act * (1.0 - sigmoid_z))).astype(jnp.bfloat16)
    grad_a = jnp.dot(normed_low.T, grad_pre, preferred_element_type=jnp.float32)
    grad_normed = jnp.dot(grad_pre, weight_a.T, preferred_element_type=jnp.float32)
    grad_input = grad_out.astype(jnp.float32) + inv_rms * (grad_normed - normed * lax.optimization_barrier(jnp.mean(grad_normed * normed, axis=-1, keepdims=True)))
    return (grad_input.astype(jnp.bfloat16), grad_a, grad_b)

def reference(pixels, cotangent, weights_a, weights_b):
    pipe_count = N_PIPE
    section_count = 2 * pipe_count

    def where_of(section):
        if section < pipe_count:
            return (0, section)
        return (1, section_count - 1 - section)
    sums_a = {}
    sums_b = {}
    for section in range(section_count):
        sums_a[section] = jnp.zeros((C, C), jnp.float32)
        sums_b[section] = jnp.zeros((C, C), jnp.float32)
    for batch in range(M):
        current = pixels[batch]
        enc_outputs = []
        saved_list = []
        for section in range(pipe_count):
            side, spot = where_of(section)
            current, saved = run_block(current.astype(jnp.float32), weights_a[side, spot], weights_b[side, spot])
            enc_outputs.append(current)
            saved_list.append(saved)
        flowing = current
        for section in range(pipe_count, section_count):
            side, spot = where_of(section)
            skip_in = enc_outputs[section_count - 1 - section]
            flowing, saved = run_block(flowing.astype(jnp.float32) + skip_in.astype(jnp.float32), weights_a[side, spot], weights_b[side, spot])
            saved_list.append(saved)
        grad_now = cotangent[batch]
        skip_grads = {}
        for section in range(section_count - 1, pipe_count - 1, -1):
            side, spot = where_of(section)
            grad_now, grad_a, grad_b = back_block(grad_now, saved_list[section], weights_a[side, spot], weights_b[side, spot])
            sums_a[section] = sums_a[section] + grad_a
            sums_b[section] = sums_b[section] + grad_b
            skip_grads[section_count - 1 - section] = grad_now
        for section in range(pipe_count - 1, -1, -1):
            side, spot = where_of(section)
            grad_out = (grad_now.astype(jnp.float32) + skip_grads[section].astype(jnp.float32)).astype(jnp.bfloat16)
            grad_now, grad_a, grad_b = back_block(grad_out, saved_list[section], weights_a[side, spot], weights_b[side, spot])
            sums_a[section] = sums_a[section] + grad_a
            sums_b[section] = sums_b[section] + grad_b
    factor = 1.0 / math.sqrt(M * TOKENS)
    enc_a = jnp.stack([sums_a[section] for section in range(pipe_count)])
    dec_a = jnp.stack([sums_a[section_count - 1 - spot] for spot in range(pipe_count)])
    enc_b = jnp.stack([sums_b[section] for section in range(pipe_count)])
    dec_b = jnp.stack([sums_b[section_count - 1 - spot] for spot in range(pipe_count)])
    return (jnp.stack([enc_a, dec_a]) * factor, jnp.stack([enc_b, dec_b]) * factor)
```

```python
import functools
import math

import jax
import jax.numpy as jnp
from jax import lax
from jax.experimental import pallas as pl
from jax.experimental.pallas import tpu as pltpu
from jax.sharding import PartitionSpec as P

EPS = 1e-06
LEVELS = 4
ROWS = 32
WIDTH = 512
HALF = WIDTH // 2
BF16 = jnp.bfloat16
F32 = jnp.float32
VMEM_BYTES = 48 * 1024 * 1024


def dot(a, b):
    return jnp.dot(a, b, preferred_element_type=F32)


def dot_t(a, b):
    return lax.dot_general(a, b, (((1,), (1,)), ((), ())), preferred_element_type=F32)


def t_dot(a, b):
    return lax.dot_general(a, b, (((0,), (0,)), ((), ())), preferred_element_type=F32)


def forward_level(v, weight, save, slot):
    save_q, save_z, save_r = save
    r = lax.rsqrt(jnp.mean(v * v, axis=-1, keepdims=True) + EPS)
    q = v * r
    z = dot(q.astype(BF16), weight[0])
    h = (z * jax.nn.sigmoid(z)).astype(BF16)
    save_q[slot] = q
    save_z[slot] = z
    save_r[slot] = jnp.broadcast_to(r, (ROWS, 128))
    return (v + dot(h, weight[1])).astype(BF16)


def backward_level(g, weight, save, slot, acts, last=False):
    save_q, save_z, save_r = save
    gh = dot_t(g, weight[1])
    z = save_z[slot]
    s = jax.nn.sigmoid(z)
    gz = (gh * s * (1.0 + z * (1.0 - s))).astype(BF16)
    q = save_q[slot]
    acts[slot, 0] = q.astype(BF16)
    acts[slot, 1] = gz
    acts[slot, 2] = (z * s).astype(BF16)
    acts[slot, 3] = g
    gn = dot_t(gz, weight[0])
    r = save_r[slot][:, :1]
    return (g.astype(F32) + r * (gn - q * jnp.mean(gn * q, axis=-1, keepdims=True))).astype(BF16)


def start_weights(place, weights, side, held, sems, order):
    own_a, own_b, *pieces = weights
    both = pl.ds(2 * side, 2)
    near = (pieces[0].at[both], pieces[2].at[both], pieces[4 + 2 * side])
    far = (pieces[1].at[both], pieces[3].at[both], pieces[5 + 2 * side])

    def start(m, apart):
        if apart == 0:
            pltpu.make_async_copy(own_a.at[side, 0], held.at[m, 0], sems.at[m]).start()
            pltpu.make_async_copy(own_b.at[side, 0], held.at[m, 1], sems.at[m]).start()
            return
        for part, core in ((near[apart - 1], place[2]), (far[apart - 1], 1 - place[2])):
            rows = pl.ds(pl.multiple_of(core * HALF, HALF), HALF)
            pltpu.make_async_copy(part, held.at[m, :, rows, :], sems.at[m]).start()

    for m in order:
        for apart in range(LEVELS):
            pl.when(place[1] == (m ^ apart))(functools.partial(start, m, apart))


def wait_weights(held, sems, m):
    pltpu.make_async_copy(held.at[m], held.at[m], sems.at[m]).wait()
    return held.at[m]


UP = tuple(range(LEVELS))
DOWN = tuple(reversed(UP))
N_WEIGHTS = 10


def own_level_kernel(level, place, x, own_a, own_b, out, held, sems):
    @pl.when(place[3] == level)
    def _():
        copies = [
            pltpu.make_async_copy(own.at[0, 0], held.at[i], sems.at[i]) for i, own in enumerate((own_a, own_b))
        ]
        for copy in copies:
            copy.start()
        v = x[...].reshape(LEVELS * ROWS, WIDTH).astype(F32)
        n = (v * lax.rsqrt(jnp.mean(v * v, axis=-1, keepdims=True) + EPS)).astype(BF16)
        copies[0].wait()
        z = dot(n, held[0])
        h = (z * jax.nn.sigmoid(z)).astype(BF16)
        copies[1].wait()
        out[...] = (v + dot(h, held[1])).astype(BF16).reshape(LEVELS, ROWS, WIDTH)


def forward_kernel(place, pixels, *refs):
    arrived, weights, refs = refs[:LEVELS], refs[LEVELS : LEVELS + N_WEIGHTS], refs[LEVELS + N_WEIGHTS :]
    hop, e, qe, ze, re, qd, zd, rd, held_e, held_d, sems_e, sems_d = refs
    late = place[0] == 1
    start_weights(place, weights, 0, held_e, sems_e, UP)
    pl.when(late)(lambda: start_weights(place, weights, 1, held_d, sems_d, DOWN))
    x = jnp.where(late, sum(a[...].astype(F32) for a in arrived), pixels[place[1]].astype(F32))
    for m in UP:
        x = forward_level(x.astype(F32), wait_weights(held_e, sems_e, m), (qe, ze, re), m)
        e[m] = x

    @pl.when(late)
    def _():
        d = e[LEVELS - 1]
        for m in DOWN:
            v = d.astype(F32) + e[m].astype(F32)
            d = forward_level(v, wait_weights(held_d, sems_d, m), (qd, zd, rd), m)
        hop[...] = d


def turn_dec_kernel(place, arrived, e, cotangent, *refs):
    weights, refs = refs[:N_WEIGHTS], refs[N_WEIGHTS:]
    hop, skip_grads, acts, held, sems, q, z, r, local_acts, acts_sem = refs

    @pl.when(place[0] == 0)
    def _():
        start_weights(place, weights, 1, held, sems, DOWN)
        x = arrived[...]
        for m in DOWN:
            v = x.astype(F32) + e[m].astype(F32)
            x = forward_level(v, wait_weights(held, sems, m), (q, z, r), m)
        g = cotangent[place[1]]
        for m in UP:
            g = backward_level(g, held.at[m], (q, z, r), m, local_acts)
            skip_grads[m] = g
        hop[...] = g
        out = pltpu.make_async_copy(local_acts, acts.at[:, 1], acts_sem)
        out.start()
        out.wait()


def enc_backward(g, skip_grads, weights, save, acts):
    for m in DOWN:
        g = (g.astype(F32) + skip_grads[m].astype(F32)).astype(BF16)
        g = backward_level(g, weights(m), save, m, acts)
    return g


def turn_backward_kernel(place, arrived, qe, ze, re, qd, zd, rd, *refs):
    weights, refs = refs[:N_WEIGHTS], refs[N_WEIGHTS + 1 :]
    hop, acts, held_e, held_d, sems_e, sems_d, acts_e, acts_d, acts_sems = refs

    @pl.when(place[0] == 1)
    def _():
        start_weights(place, weights, 1, held_d, sems_d, UP)
        start_weights(place, weights, 0, held_e, sems_e, DOWN)
        g = arrived[...]
        skip_grads = []
        for m in UP:
            g = backward_level(g, wait_weights(held_d, sems_d, m), (qd, zd, rd), m, acts_d)
            skip_grads.append(g)
        out_d = pltpu.make_async_copy(acts_d, acts.at[:, 1], acts_sems.at[1])
        out_d.start()
        hop[...] = enc_backward(
            g, skip_grads, lambda m: wait_weights(held_e, sems_e, m), (qe, ze, re), acts_e
        )
        out_e = pltpu.make_async_copy(acts_e, acts.at[:, 0], acts_sems.at[0])
        out_e.start()
        out_d.wait()
        out_e.wait()


def enc_backward_kernel(place, arrived, q, z, r, skip_grads, *refs):
    weights, refs = refs[:N_WEIGHTS], refs[N_WEIGHTS + 1 :]
    acts, held, sems, local_acts, acts_sem = refs

    @pl.when(place[0] == 0)
    def _():
        start_weights(place, weights, 0, held, sems, DOWN)
        enc_backward(
            arrived[...], skip_grads, lambda m: wait_weights(held, sems, m), (q, z, r), local_acts
        )
        out = pltpu.make_async_copy(local_acts, acts.at[:, 0], acts_sem)
        out.start()
        out.wait()


def grads_kernel(acts, out):
    rows = acts.shape[0] * ROWS
    grad = t_dot(acts[:, 0].reshape(rows, WIDTH), acts[:, 1].reshape(rows, WIDTH))
    for z_low in range(4):
        for z_high in range(4):
            for x in range(2):
                for core in range(2):
                    first = x * 256 + (z_high * 4 + z_low) * 16 + core * 8
                    out[z_low, x, core, z_high] = grad[first : first + 8].astype(BF16)


SMEM = pl.BlockSpec(memory_space=pltpu.SMEM)
VMEM = pl.BlockSpec(memory_space=pltpu.VMEM)
ANY = pl.BlockSpec(memory_space=pl.ANY)
PARAMS = pltpu.CompilerParams(vmem_limit_bytes=VMEM_BYTES)

ROW = jax.ShapeDtypeStruct((ROWS, WIDTH), BF16)
STACK = jax.ShapeDtypeStruct((LEVELS, ROWS, WIDTH), BF16)
SAVE = jax.ShapeDtypeStruct((LEVELS, ROWS, WIDTH), F32)
SAVE_R = jax.ShapeDtypeStruct((LEVELS, ROWS, 128), F32)
SAVES = (SAVE, SAVE, SAVE_R)
ACTS = jax.ShapeDtypeStruct((LEVELS, 2, 4, ROWS, WIDTH), BF16)

HELD = pltpu.VMEM((LEVELS, 2, WIDTH, WIDTH), BF16)
SEMS = pltpu.SemaphoreType.DMA((LEVELS,))
LOCAL_ACTS = pltpu.VMEM((LEVELS, 4, ROWS, WIDTH), BF16)
SCRATCH_SAVES = tuple(pltpu.VMEM(s.shape, s.dtype) for s in SAVES)


def call(kernel, operands, spaces, outs, out_spaces, scratch=(), aliases=None, name=None):
    return pl.pallas_call(
        kernel,
        out_shape=outs,
        in_specs=spaces,
        out_specs=out_spaces,
        scratch_shapes=scratch,
        input_output_aliases=aliases or {},
        compiler_params=PARAMS,
        name=name,
    )(*operands)


def local(pixels, cotangent, weights_a, weights_b):
    core = lax.axis_index("core")
    level = lax.axis_index(PIPE)
    place = jnp.stack([level // LEVELS, level % LEVELS, core, level]).astype(jnp.int32)

    half = jnp.stack(
        [
            lax.dynamic_slice_in_dim(w[side, 0], core * HALF, HALF, 0)
            for side in (0, 1)
            for w in (weights_a, weights_b)
        ]
    )

    def along_x(block):
        return lax.ppermute(block, ("x_lo", "x_hi"), [(i, 3 - i) for i in range(4)])

    def along_y(block):
        return lax.ppermute(block, "y_lo", [(0, 1), (1, 0)])

    from_x = along_x(half)
    from_y = along_y(half)

    x = pixels
    for k in range(LEVELS):
        if k:
            x = lax.ppermute(x, PIPE, [(k - 1, k)])
        x = call(
            functools.partial(own_level_kernel, k), (place, x, weights_a, weights_b), (SMEM, VMEM, ANY, ANY),
            STACK, VMEM, (pltpu.VMEM((2, WIDTH, WIDTH), BF16), pltpu.SemaphoreType.DMA((2,))), name="own_level",
        )
    x, from_x, from_y = lax.optimization_barrier((x, from_x, from_y))

    pieces = [from_x, from_y, along_y(from_x[:2]), along_x(from_y[2:])]
    pieces = [v for piece in pieces for v in (piece, lax.ppermute(piece, "core", [(0, 1), (1, 0)]))]
    weights = (weights_a, weights_b, *pieces)

    up = [(0, 3), (1, 2)]
    down = [(3, 0), (2, 1)]
    y = ("stage", "y_lo")
    arrived = [lax.ppermute(x[j], PIPE, [(LEVELS - 1, (3 - j // 2) * 2 + j % 2)]) for j in range(LEVELS)]

    hop, e, *saves = call(
        forward_kernel, (place, pixels, *arrived, *weights), (SMEM,) + (VMEM,) * 5 + (ANY,) * N_WEIGHTS,
        (ROW, STACK) + SAVES + SAVES, (VMEM,) * 8, (HELD, HELD, SEMS, SEMS), name="forward",
    )
    arrived = lax.ppermute(hop, y, down)
    hop, skip_grads, acts = call(
        turn_dec_kernel, (place, arrived, e, cotangent, *weights),
        (SMEM, VMEM, VMEM, VMEM) + (ANY,) * N_WEIGHTS,
        (ROW, STACK, ACTS), (VMEM, VMEM, ANY),
        (HELD, SEMS) + SCRATCH_SAVES + (LOCAL_ACTS, pltpu.SemaphoreType.DMA), name="turn_dec",
    )
    arrived = lax.ppermute(hop, y, up)
    hop, acts = call(
        turn_backward_kernel, (place, arrived, *saves, *weights, acts),
        (SMEM, VMEM) + (VMEM,) * 6 + (ANY,) * (N_WEIGHTS + 1),
        (ROW, ACTS), (VMEM, ANY),
        (HELD, HELD, SEMS, SEMS, LOCAL_ACTS, LOCAL_ACTS, pltpu.SemaphoreType.DMA((2,))),
        {8 + N_WEIGHTS: 1}, name="turn_backward",
    )
    arrived = lax.ppermute(hop, y, down)
    acts = call(
        enc_backward_kernel, (place, arrived, *saves[:3], skip_grads, *weights, acts),
        (SMEM, VMEM) + (VMEM,) * 4 + (ANY,) * (N_WEIGHTS + 1),
        ACTS, ANY, (HELD, SEMS, LOCAL_ACTS, pltpu.SemaphoreType.DMA), {6 + N_WEIGHTS: 0}, name="enc_backward",
    )

    acts = lax.all_to_all(acts.reshape(16, 2, ROWS, WIDTH), MEMBERS + ("x_lo", "core"), 0, 0)
    grad = call(
        grads_kernel, (acts,), (VMEM,), jax.ShapeDtypeStruct((4, 2, 2, 4, 8, WIDTH), BF16), VMEM, name="grads"
    )

    total = lax.all_to_all(grad.reshape(16, 4, 8, WIDTH), ("z_lo", "x_lo", "core"), 0, 0)
    total = jnp.sum(total.astype(F32).reshape(4, 4, 4, 8, WIDTH), axis=0).astype(BF16)
    total = lax.all_to_all(total.transpose(1, 0, 2, 3), "z_hi", 0, 0)
    factor = 1.0 / math.sqrt(LEVELS * ROWS * 64)
    total = jnp.sum(total.astype(F32), axis=0).reshape(2, 2, 1, 8, WIDTH) * factor
    return total[:, 0], total[:, 1]


MEMBERS = ("y_lo", "x_hi")
DP = ("x_lo", "z_hi", "z_lo", "core")
PIPE = ("stage", "y_lo", "x_hi")


def solution(mesh):
    fine = jax.sharding.Mesh(mesh.devices.reshape(2, 4, 4, 2, 2, 2, 2), DP + PIPE)
    return jax.shard_map(
        local,
        mesh=fine,
        in_specs=(
            P(None, DP, None),
            P(None, DP, None),
            P(None, PIPE, None, None),
            P(None, PIPE, None, None),
        ),
        out_specs=(P(None, PIPE, DP, None), P(None, PIPE, DP, None)),
        check_vma=False,
    )
```

```python
import functools
import math

import jax
import jax.numpy as jnp
from jax import lax
from jax.experimental import pallas as pl
from jax.experimental.pallas import tpu as pltpu
from jax.sharding import PartitionSpec as P

EPS = 1e-06
LEVELS = 4
ROWS = 32
WIDTH = 512
HALF = WIDTH // 2
BF16 = jnp.bfloat16
F32 = jnp.float32
VMEM_BYTES = 26 * 1024 * 1024


def dot(a, b):
    return jnp.dot(a, b, preferred_element_type=F32)


def dot_t(a, b):
    return lax.dot_general(a, b, (((1,), (1,)), ((), ())), preferred_element_type=F32)


def t_dot(a, b):
    return lax.dot_general(a, b, (((0,), (0,)), ((), ())), preferred_element_type=F32)


def forward_level(v, weight, save, slot):
    save_q, save_z, save_r = save
    r = lax.rsqrt(jnp.mean(v * v, axis=-1, keepdims=True) + EPS)
    q = v * r
    z = dot(q.astype(BF16), weight[0])
    h = (z * jax.nn.sigmoid(z)).astype(BF16)
    save_q[slot] = q
    save_z[slot] = z
    save_r[slot] = jnp.broadcast_to(r, (ROWS, 128))
    return (v + dot(h, weight[1])).astype(BF16)


def backward_level(g, weight, save, slot, acts, first=False):
    save_q, save_z, save_r = save
    gh = dot_t(g, weight[1])
    z = save_z[slot]
    s = jax.nn.sigmoid(z)
    gz = (gh * s * (1.0 + z * (1.0 - s))).astype(BF16)
    q = save_q[slot]
    acts[slot, 0] = q.astype(BF16)
    acts[slot, 1] = gz
    acts[slot, 2] = (z * s).astype(BF16)
    acts[slot, 3] = g
    if first:
        return None
    gn = dot_t(gz, weight[0])
    r = save_r[slot][:, :1]
    return (g.astype(F32) + r * (gn - q * jnp.mean(gn * q, axis=-1, keepdims=True))).astype(BF16)


def own_weights_kernel(place, own_a, own_b, half_e, half_d, held_e, held_d, sems):
    rows = pl.ds(pl.multiple_of(place[2] * HALF, HALF), HALF)
    copies = []
    for side, (half, held) in enumerate(((half_e, held_e), (half_d, held_d))):
        for i, own in enumerate((own_a, own_b)):
            copies.append(pltpu.make_async_copy(own.at[side, 0, rows, :], half.at[i], sems.at[len(copies)]))
            copies.append(pltpu.make_async_copy(own.at[side, 0], held.at[place[1], i], sems.at[len(copies)]))
    for copy in copies:
        copy.start()
    for copy in copies:
        copy.wait()


def start_weights(place, pieces, held, sems, order):
    def start(m, apart):
        for part, core in ((pieces[2 * apart - 2], place[2]), (pieces[2 * apart - 1], 1 - place[2])):
            rows = pl.ds(pl.multiple_of(core * HALF, HALF), HALF)
            pltpu.make_async_copy(part, held.at[m, :, rows, :], sems.at[m]).start()

    for m in order:
        for apart in range(1, LEVELS):
            pl.when(place[1] == (m ^ apart))(functools.partial(start, m, apart))


def wait_weights(place, held, sems, m):
    pl.when(place[1] != m)(pltpu.make_async_copy(held.at[m], held.at[m], sems.at[m]).wait)
    return held.at[m]


N_PIECES = 6


UP = tuple(range(LEVELS))
DOWN = tuple(reversed(UP))


def enc_forward_kernel(place, pixels, *refs):
    pieces, (_, hop, e, q, z, r, held, sems) = refs[:N_PIECES], refs[N_PIECES:]
    start_weights(place, pieces, held, sems, UP)

    @pl.when(place[0] == 0)
    def _():
        x = pixels[place[1]]
        for m in UP:
            x = forward_level(x.astype(F32), wait_weights(place, held, sems, m), (q, z, r), m)
            e[m] = x
        hop[...] = x

    @pl.when(place[0] != 0)
    def _():
        for m in UP:
            wait_weights(place, held, sems, m)


def turn_forward_kernel(place, arrived, weights_e, *refs):
    pieces, (_, hop, qe, ze, re, qd, zd, rd, held, sems) = refs[:N_PIECES], refs[N_PIECES:]
    start_weights(place, pieces, held, sems, DOWN)

    @pl.when(place[0] == 1)
    def _():
        x = arrived[...]
        skips = []
        for m in UP:
            x = forward_level(x.astype(F32), weights_e.at[m], (qe, ze, re), m)
            skips.append(x)
        for m in DOWN:
            v = x.astype(F32) + skips[m].astype(F32)
            x = forward_level(v, wait_weights(place, held, sems, m), (qd, zd, rd), m)
        hop[...] = x

    @pl.when(place[0] != 1)
    def _():
        for m in DOWN:
            wait_weights(place, held, sems, m)


def turn_dec_kernel(
    place, arrived, e, cotangent, weights, hop, skip_grads, acts, q, z, r, local_acts, acts_sem
):
    @pl.when(place[0] == 0)
    def _():
        x = arrived[...]
        for m in DOWN:
            v = x.astype(F32) + e[m].astype(F32)
            x = forward_level(v, weights.at[m], (q, z, r), m)
        g = cotangent[place[1]]
        for m in UP:
            g = backward_level(g, weights.at[m], (q, z, r), m, local_acts)
            skip_grads[m] = g
        hop[...] = g
        out = pltpu.make_async_copy(local_acts, acts.at[:, 1], acts_sem)
        out.start()
        out.wait()


def enc_backward(g, skip_grads, weights, save, acts, first=False):
    for m in DOWN:
        g = (g.astype(F32) + skip_grads[m].astype(F32)).astype(BF16)
        g = backward_level(g, weights.at[m], save, m, acts, first and m == 0)
    return g


def turn_backward_kernel(
    place, arrived, qe, ze, re, qd, zd, rd, weights_e, weights_d, acts_in, hop, acts, acts_e, acts_d, acts_sems
):
    del acts_in

    @pl.when(place[0] == 1)
    def _():
        g = arrived[...]
        skip_grads = []
        for m in UP:
            g = backward_level(g, weights_d.at[m], (qd, zd, rd), m, acts_d)
            skip_grads.append(g)
        out_d = pltpu.make_async_copy(acts_d, acts.at[:, 1], acts_sems.at[1])
        out_d.start()
        hop[...] = enc_backward(g, skip_grads, weights_e, (qe, ze, re), acts_e)
        out_e = pltpu.make_async_copy(acts_e, acts.at[:, 0], acts_sems.at[0])
        out_e.start()
        out_d.wait()
        out_e.wait()


def enc_backward_kernel(place, arrived, q, z, r, skip_grads, weights, acts_in, acts, local_acts, acts_sem):
    del acts_in

    @pl.when(place[0] == 0)
    def _():
        enc_backward(arrived[...], skip_grads, weights, (q, z, r), local_acts, first=True)
        out = pltpu.make_async_copy(local_acts, acts.at[:, 0], acts_sem)
        out.start()
        out.wait()


def grads_kernel(acts, out):
    rows = acts.shape[0] * ROWS
    grad = t_dot(acts[:, 0].reshape(rows, WIDTH), acts[:, 1].reshape(rows, WIDTH))
    for z_low in range(4):
        for z_high in range(4):
            for x in range(2):
                for core in range(2):
                    first = x * 256 + (z_high * 4 + z_low) * 16 + core * 8
                    out[z_low, x, core, z_high] = grad[first : first + 8].astype(BF16)


SMEM = pl.BlockSpec(memory_space=pltpu.SMEM)
VMEM = pl.BlockSpec(memory_space=pltpu.VMEM)
ANY = pl.BlockSpec(memory_space=pl.ANY)
PARAMS = pltpu.CompilerParams(vmem_limit_bytes=VMEM_BYTES)

ROW = jax.ShapeDtypeStruct((ROWS, WIDTH), BF16)
STACK = jax.ShapeDtypeStruct((LEVELS, ROWS, WIDTH), BF16)
SAVE = jax.ShapeDtypeStruct((LEVELS, ROWS, WIDTH), F32)
SAVE_R = jax.ShapeDtypeStruct((LEVELS, ROWS, 128), F32)
SAVES = (SAVE, SAVE, SAVE_R)
ACTS = jax.ShapeDtypeStruct((LEVELS, 2, 4, ROWS, WIDTH), BF16)

WEIGHTS = jax.ShapeDtypeStruct((LEVELS, 2, WIDTH, WIDTH), BF16)

SEMS = pltpu.SemaphoreType.DMA((LEVELS,))
LOCAL_ACTS = pltpu.VMEM((LEVELS, 4, ROWS, WIDTH), BF16)
SCRATCH_SAVES = tuple(pltpu.VMEM(s.shape, s.dtype) for s in SAVES)


def call(kernel, operands, spaces, outs, out_spaces, scratch=(), aliases=None, name=None):
    return pl.pallas_call(
        kernel,
        out_shape=outs,
        in_specs=spaces,
        out_specs=out_spaces,
        scratch_shapes=scratch,
        input_output_aliases=aliases or {},
        compiler_params=PARAMS,
        name=name,
    )(*operands)


def local(pixels, cotangent, weights_a, weights_b):
    core = lax.axis_index("core")
    level = lax.axis_index(PIPE)
    place = jnp.stack([level // LEVELS, level % LEVELS, core, level]).astype(jnp.int32)

    piece = jax.ShapeDtypeStruct((2, HALF, WIDTH), BF16)
    half_e, half_d, own_e, own_d = call(
        own_weights_kernel, (place, weights_a, weights_b), (SMEM, ANY, ANY), (piece, piece, WEIGHTS, WEIGHTS),
        (VMEM,) * 4, (pltpu.SemaphoreType.DMA((8,)),), name="own_weights",
    )

    def along_x(block):
        return lax.ppermute(block, ("x_lo", "x_hi"), [(i, 3 - i) for i in range(4)])

    def along_y(block):
        return lax.ppermute(block, "y_lo", [(0, 1), (1, 0)])

    def swap(block):
        return lax.ppermute(block, "core", [(0, 1), (1, 0)])

    x_e, y_d = along_x(half_e), along_y(half_d)
    x_d, y_e = along_x(half_d), along_y(half_e)
    diagonal_e, diagonal_d = along_y(x_e), along_x(y_d)

    pieces = []
    for piece in (x_e, y_e, diagonal_e, x_d, y_d):
        pieces += [piece, swap(piece)]
    *pieces, diagonal_d = lax.optimization_barrier((*pieces, diagonal_d))

    up = [(0, 3), (1, 2)]
    down = [(3, 0), (2, 1)]
    y = ("stage", "y_lo")

    hop, e, *saves_0, weights_e = call(
        enc_forward_kernel, (place, pixels, *pieces[:6], own_e), (SMEM, VMEM) + (ANY,) * N_PIECES + (VMEM,),
        (ROW, STACK) + SAVES + (WEIGHTS,), (VMEM,) * 6, (SEMS,), {2 + N_PIECES: 5}, name="enc_forward",
    )
    hop, diagonal_d = lax.optimization_barrier((hop, diagonal_d))
    arrived = lax.ppermute(hop, y, up)
    pieces = (*pieces[6:], diagonal_d, swap(diagonal_d))
    hop, *saves, weights_d = call(
        turn_forward_kernel, (place, arrived, weights_e, *pieces, own_d),
        (SMEM, VMEM, VMEM) + (ANY,) * N_PIECES + (VMEM,),
        (ROW,) + SAVES + SAVES + (WEIGHTS,), (VMEM,) * 8, (SEMS,), {3 + N_PIECES: 7}, name="turn_forward",
    )
    arrived = lax.ppermute(hop, y, down)
    hop, skip_grads, acts = call(
        turn_dec_kernel, (place, arrived, e, cotangent, weights_d), (SMEM,) + (VMEM,) * 4,
        (ROW, STACK, ACTS), (VMEM, VMEM, ANY),
        SCRATCH_SAVES + (LOCAL_ACTS, pltpu.SemaphoreType.DMA), name="turn_dec",
    )
    arrived = lax.ppermute(hop, y, up)
    hop, acts = call(
        turn_backward_kernel, (place, arrived, *saves, weights_e, weights_d, acts), (SMEM,) + (VMEM,) * 9 + (ANY,),
        (ROW, ACTS), (VMEM, ANY),
        (LOCAL_ACTS, LOCAL_ACTS, pltpu.SemaphoreType.DMA((2,))), {10: 1}, name="turn_backward",
    )
    arrived = lax.ppermute(hop, y, down)
    acts = call(
        enc_backward_kernel, (place, arrived, *saves_0, skip_grads, weights_e, acts), (SMEM,) + (VMEM,) * 6 + (ANY,),
        ACTS, ANY, (LOCAL_ACTS, pltpu.SemaphoreType.DMA), {7: 0}, name="enc_backward",
    )

    acts = lax.all_to_all(acts.reshape(16, 2, ROWS, WIDTH), MEMBERS + ("x_lo", "core"), 0, 0)
    grad = call(
        grads_kernel, (acts,), (VMEM,), jax.ShapeDtypeStruct((4, 2, 2, 4, 8, WIDTH), BF16), VMEM, name="grads"
    )

    total = lax.all_to_all(grad.reshape(16, 4, 8, WIDTH), ("z_lo", "x_lo", "core"), 0, 0)
    total = jnp.sum(total.astype(F32).reshape(4, 4, 4, 8, WIDTH), axis=0).astype(BF16)
    total = lax.all_to_all(total.transpose(1, 0, 2, 3), "z_hi", 0, 0)
    factor = 1.0 / math.sqrt(LEVELS * ROWS * 64)
    total = jnp.sum(total.astype(F32), axis=0).reshape(2, 2, 1, 8, WIDTH) * factor
    return total[:, 0], total[:, 1]


MEMBERS = ("y_lo", "x_hi")
DP = ("x_lo", "z_hi", "z_lo", "core")
PIPE = ("stage", "y_lo", "x_hi")


def solution(mesh):
    fine = jax.sharding.Mesh(mesh.devices.reshape(2, 4, 4, 2, 2, 2, 2), DP + PIPE)
    return jax.shard_map(
        local,
        mesh=fine,
        in_specs=(
            P(None, DP, None),
            P(None, DP, None),
            P(None, PIPE, None, None),
            P(None, PIPE, None, None),
        ),
        out_specs=(P(None, PIPE, DP, None), P(None, PIPE, DP, None)),
        check_vma=False,
    )
```

```python
import functools
import math

import jax
import jax.numpy as jnp
from jax import lax
from jax.experimental import pallas as pl
from jax.experimental.pallas import tpu as pltpu
from jax.sharding import PartitionSpec as P

EPS = 1e-06
LEVELS = 4
ROWS = 32
WIDTH = 512
HALF = WIDTH // 2
BF16 = jnp.bfloat16
F32 = jnp.float32
VMEM_BYTES = 26 * 1024 * 1024


def dot(a, b):
    return jnp.dot(a, b, preferred_element_type=F32)


def dot_t(a, b):
    return lax.dot_general(a, b, (((1,), (1,)), ((), ())), preferred_element_type=F32)


def t_dot(a, b):
    return lax.dot_general(a, b, (((0,), (0,)), ((), ())), preferred_element_type=F32)


def forward_level(v, weight, save, slot):
    save_q, save_z, save_r = save
    r = lax.rsqrt(jnp.mean(v * v, axis=-1, keepdims=True) + EPS)
    q = v * r
    z = dot(q.astype(BF16), weight[0])
    h = (z * jax.nn.sigmoid(z)).astype(BF16)
    save_q[slot] = q
    save_z[slot] = z
    save_r[slot] = jnp.broadcast_to(r, (ROWS, 128))
    return (v + dot(h, weight[1])).astype(BF16)


def backward_level(g, weight, save, slot, acts, side, first=False):
    save_q, save_z, save_r = save
    gh = dot_t(g, weight[1])
    z = save_z[slot]
    s = jax.nn.sigmoid(z)
    gz = (gh * s * (1.0 + z * (1.0 - s))).astype(BF16)
    q = save_q[slot]
    acts[slot, side, 0] = q.astype(BF16)
    acts[slot, side, 1] = gz
    acts[slot, side, 2] = (z * s).astype(BF16)
    acts[slot, side, 3] = g
    if first:
        return None
    gn = dot_t(gz, weight[0])
    r = save_r[slot][:, :1]
    return (g.astype(F32) + r * (gn - q * jnp.mean(gn * q, axis=-1, keepdims=True))).astype(BF16)


def own_weights_kernel(place, own_a, own_b, half_e, half_d, held_e, held_d, sems):
    rows = pl.ds(pl.multiple_of(place[2] * HALF, HALF), HALF)
    copies = []
    for side, (half, held) in enumerate(((half_e, held_e), (half_d, held_d))):
        for i, own in enumerate((own_a, own_b)):
            copies.append(pltpu.make_async_copy(own.at[side, 0, rows, :], half.at[i], sems.at[len(copies)]))
            copies.append(pltpu.make_async_copy(own.at[side, 0], held.at[place[1], i], sems.at[len(copies)]))
    for copy in copies:
        copy.start()
    for copy in copies:
        copy.wait()


def start_weights(place, pieces, held, sems, order):
    def start(m, apart):
        for part, core in ((pieces[2 * apart - 2], place[2]), (pieces[2 * apart - 1], 1 - place[2])):
            rows = pl.ds(pl.multiple_of(core * HALF, HALF), HALF)
            pltpu.make_async_copy(part, held.at[m, :, rows, :], sems.at[m]).start()

    for m in order:
        for apart in range(1, LEVELS):
            pl.when(place[1] == (m ^ apart))(functools.partial(start, m, apart))


def wait_weights(place, held, sems, m):
    pl.when(place[1] != m)(pltpu.make_async_copy(held.at[m], held.at[m], sems.at[m]).wait)
    return held.at[m]


N_PIECES = 6


UP = tuple(range(LEVELS))
DOWN = tuple(reversed(UP))


def enc_forward_kernel(place, pixels, *refs):
    pieces, (_, hop, e, q, z, r, held, sems) = refs[:N_PIECES], refs[N_PIECES:]
    start_weights(place, pieces, held, sems, UP)

    @pl.when(place[0] == 0)
    def _():
        x = pixels[place[1]]
        for m in UP:
            x = forward_level(x.astype(F32), wait_weights(place, held, sems, m), (q, z, r), m)
            e[m] = x
        hop[...] = x

    @pl.when(place[0] != 0)
    def _():
        for m in UP:
            wait_weights(place, held, sems, m)


def turn_forward_kernel(place, arrived, weights_e, *refs):
    pieces, (_, hop, qe, ze, re, qd, zd, rd, held, sems) = refs[:N_PIECES], refs[N_PIECES:]
    start_weights(place, pieces, held, sems, DOWN)

    @pl.when(place[0] == 1)
    def _():
        x = arrived[...]
        skips = []
        for m in UP:
            x = forward_level(x.astype(F32), weights_e.at[m], (qe, ze, re), m)
            skips.append(x)
        for m in DOWN:
            v = x.astype(F32) + skips[m].astype(F32)
            x = forward_level(v, wait_weights(place, held, sems, m), (qd, zd, rd), m)
        hop[...] = x

    @pl.when(place[0] != 1)
    def _():
        for m in DOWN:
            wait_weights(place, held, sems, m)


def turn_dec_kernel(place, arrived, e, cotangent, weights, hop, skip_grads, acts, q, z, r):
    @pl.when(place[0] == 0)
    def _():
        x = arrived[...]
        for m in DOWN:
            v = x.astype(F32) + e[m].astype(F32)
            x = forward_level(v, weights.at[m], (q, z, r), m)
        g = cotangent[place[1]]
        for m in UP:
            g = backward_level(g, weights.at[m], (q, z, r), m, acts, 1)
            skip_grads[m] = g
        hop[...] = g


def enc_backward(g, skip_grads, weights, save, acts, first=False):
    for m in DOWN:
        g = (g.astype(F32) + skip_grads[m].astype(F32)).astype(BF16)
        g = backward_level(g, weights.at[m], save, m, acts, 0, first and m == 0)
    return g


def turn_backward_kernel(place, arrived, qe, ze, re, qd, zd, rd, weights_e, weights_d, acts_in, hop, acts):
    del acts_in

    @pl.when(place[0] == 1)
    def _():
        g = arrived[...]
        skip_grads = []
        for m in UP:
            g = backward_level(g, weights_d.at[m], (qd, zd, rd), m, acts, 1)
            skip_grads.append(g)
        hop[...] = enc_backward(g, skip_grads, weights_e, (qe, ze, re), acts)


def enc_backward_kernel(place, arrived, q, z, r, skip_grads, weights, acts_in, acts):
    del acts_in

    @pl.when(place[0] == 0)
    def _():
        enc_backward(arrived[...], skip_grads, weights, (q, z, r), acts, first=True)


def grads_kernel(acts, out):
    rows = acts.shape[0] * ROWS
    grad = t_dot(acts[:, 0].reshape(rows, WIDTH), acts[:, 1].reshape(rows, WIDTH))
    for z_low in range(4):
        for z_high in range(4):
            for x in range(2):
                for core in range(2):
                    first = x * 256 + (z_high * 4 + z_low) * 16 + core * 8
                    out[z_low, x, core, z_high] = grad[first : first + 8].astype(BF16)


def last_sum_kernel(factor, parts, grads_a, grads_b):
    total = sum(parts[i].astype(F32) for i in range(4)) * factor
    for side in (0, 1):
        grads_a[side, 0] = total[2 * side]
        grads_b[side, 0] = total[2 * side + 1]


SMEM = pl.BlockSpec(memory_space=pltpu.SMEM)
VMEM = pl.BlockSpec(memory_space=pltpu.VMEM)
ANY = pl.BlockSpec(memory_space=pl.ANY)
PARAMS = pltpu.CompilerParams(vmem_limit_bytes=VMEM_BYTES)

ROW = jax.ShapeDtypeStruct((ROWS, WIDTH), BF16)
STACK = jax.ShapeDtypeStruct((LEVELS, ROWS, WIDTH), BF16)
SAVE = jax.ShapeDtypeStruct((LEVELS, ROWS, WIDTH), F32)
SAVE_R = jax.ShapeDtypeStruct((LEVELS, ROWS, 128), F32)
SAVES = (SAVE, SAVE, SAVE_R)
ACTS = jax.ShapeDtypeStruct((LEVELS, 2, 4, ROWS, WIDTH), BF16)

WEIGHTS = jax.ShapeDtypeStruct((LEVELS, 2, WIDTH, WIDTH), BF16)

SEMS = pltpu.SemaphoreType.DMA((LEVELS,))
SCRATCH_SAVES = tuple(pltpu.VMEM(s.shape, s.dtype) for s in SAVES)


def call(kernel, operands, spaces, outs, out_spaces, scratch=(), aliases=None, name=None):
    return pl.pallas_call(
        kernel,
        out_shape=outs,
        in_specs=spaces,
        out_specs=out_spaces,
        scratch_shapes=scratch,
        input_output_aliases=aliases or {},
        compiler_params=PARAMS,
        name=name,
    )(*operands)


def local(pixels, cotangent, weights_a, weights_b):
    core = lax.axis_index("core")
    level = lax.axis_index(PIPE)
    place = jnp.stack([level // LEVELS, level % LEVELS, core, level]).astype(jnp.int32)

    piece = jax.ShapeDtypeStruct((2, HALF, WIDTH), BF16)
    half_e, half_d, own_e, own_d = call(
        own_weights_kernel, (place, weights_a, weights_b), (SMEM, ANY, ANY), (piece, piece, WEIGHTS, WEIGHTS),
        (VMEM,) * 4, (pltpu.SemaphoreType.DMA((8,)),), name="own_weights",
    )

    def along_x(block):
        return lax.ppermute(block, ("x_lo", "x_hi"), [(i, 3 - i) for i in range(4)])

    def along_y(block):
        return lax.ppermute(block, "y_lo", [(0, 1), (1, 0)])

    def swap(block):
        return lax.ppermute(block, "core", [(0, 1), (1, 0)])

    x_e, y_d = along_x(half_e), along_y(half_d)
    x_d, y_e = along_x(half_d), along_y(half_e)
    diagonal_e, diagonal_d = along_y(x_e), along_x(y_d)

    pieces = []
    for piece in (x_e, y_e, diagonal_e, x_d, y_d):
        pieces += [piece, swap(piece)]
    *pieces, diagonal_d = lax.optimization_barrier((*pieces, diagonal_d))

    up = [(0, 3), (1, 2)]
    down = [(3, 0), (2, 1)]
    y = ("stage", "y_lo")

    hop, e, *saves_0, weights_e = call(
        enc_forward_kernel, (place, pixels, *pieces[:6], own_e), (SMEM, VMEM) + (ANY,) * N_PIECES + (VMEM,),
        (ROW, STACK) + SAVES + (WEIGHTS,), (VMEM,) * 6, (SEMS,), {2 + N_PIECES: 5}, name="enc_forward",
    )
    hop, diagonal_d = lax.optimization_barrier((hop, diagonal_d))
    arrived = lax.ppermute(hop, y, up)
    pieces = (*pieces[6:], diagonal_d, swap(diagonal_d))
    hop, *saves, weights_d = call(
        turn_forward_kernel, (place, arrived, weights_e, *pieces, own_d),
        (SMEM, VMEM, VMEM) + (ANY,) * N_PIECES + (VMEM,),
        (ROW,) + SAVES + SAVES + (WEIGHTS,), (VMEM,) * 8, (SEMS,), {3 + N_PIECES: 7}, name="turn_forward",
    )
    arrived = lax.ppermute(hop, y, down)
    hop, skip_grads, acts = call(
        turn_dec_kernel, (place, arrived, e, cotangent, weights_d), (SMEM,) + (VMEM,) * 4,
        (ROW, STACK, ACTS), (VMEM,) * 3, SCRATCH_SAVES, name="turn_dec",
    )
    arrived = lax.ppermute(hop, y, up)
    hop, acts = call(
        turn_backward_kernel, (place, arrived, *saves, weights_e, weights_d, acts), (SMEM,) + (VMEM,) * 10,
        (ROW, ACTS), (VMEM,) * 2, (), {10: 1}, name="turn_backward",
    )
    arrived = lax.ppermute(hop, y, down)
    acts = call(
        enc_backward_kernel, (place, arrived, *saves_0, skip_grads, weights_e, acts), (SMEM,) + (VMEM,) * 7,
        ACTS, VMEM, (), {7: 0}, name="enc_backward",
    )

    acts = lax.all_to_all(acts.reshape(16, 2, ROWS, WIDTH), MEMBERS + ("x_lo", "core"), 0, 0)
    grad = call(
        grads_kernel, (acts,), (VMEM,), jax.ShapeDtypeStruct((4, 2, 2, 4, 8, WIDTH), BF16), VMEM, name="grads"
    )

    total = lax.all_to_all(grad.reshape(16, 4, 8, WIDTH), ("z_lo", "x_lo", "core"), 0, 0)
    total = jnp.sum(total.astype(F32).reshape(4, 4, 4, 8, WIDTH), axis=0).astype(BF16)
    total = lax.all_to_all(total.transpose(1, 0, 2, 3), "z_hi", 0, 0)
    factor = 1.0 / math.sqrt(LEVELS * ROWS * 64)
    out = jax.ShapeDtypeStruct((2, 1, 8, WIDTH), F32)
    return tuple(
        call(functools.partial(last_sum_kernel, factor), (total,), (VMEM,), (out, out), (VMEM, VMEM), name="last_sum")
    )


MEMBERS = ("y_lo", "x_hi")
DP = ("x_lo", "z_hi", "z_lo", "core")
PIPE = ("stage", "y_lo", "x_hi")


def solution(mesh):
    fine = jax.sharding.Mesh(mesh.devices.reshape(2, 4, 4, 2, 2, 2, 2), DP + PIPE)
    return jax.shard_map(
        local,
        mesh=fine,
        in_specs=(
            P(None, DP, None),
            P(None, DP, None),
            P(None, PIPE, None, None),
            P(None, PIPE, None, None),
        ),
        out_specs=(P(None, PIPE, DP, None), P(None, PIPE, DP, None)),
        check_vma=False,
    )
```

```python
import functools
import math

import jax
import jax.numpy as jnp
from jax import lax
from jax.experimental import pallas as pl
from jax.experimental.pallas import tpu as pltpu
from jax.sharding import PartitionSpec as P

EPS = 1e-06
LEVELS = 4
ROWS = 32
WIDTH = 512
HALF = WIDTH // 2
BF16 = jnp.bfloat16
F32 = jnp.float32
VMEM_BYTES = 26 * 1024 * 1024


def dot(a, b):
    return jnp.dot(a, b, preferred_element_type=F32)


def dot_t(a, b):
    return lax.dot_general(a, b, (((1,), (1,)), ((), ())), preferred_element_type=F32)


def t_dot(a, b):
    return lax.dot_general(a, b, (((0,), (0,)), ((), ())), preferred_element_type=F32)


def forward_level(v, weight, save, slot):
    save_q, save_z, save_r = save
    r = lax.rsqrt(jnp.mean(v * v, axis=-1, keepdims=True) + EPS)
    q = v * r
    z = dot(q.astype(BF16), weight[0])
    h = (z * jax.nn.sigmoid(z)).astype(BF16)
    save_q[slot] = q
    save_z[slot] = z
    save_r[slot] = jnp.broadcast_to(r, (ROWS, 128))
    return (v + dot(h, weight[1])).astype(BF16)


def backward_level(g, weight, save, slot, acts, side, first=False):
    save_q, save_z, save_r = save
    gh = dot_t(g, weight[1])
    z = save_z[slot]
    s = jax.nn.sigmoid(z)
    gz = (gh * s * (1.0 + z * (1.0 - s))).astype(BF16)
    q = save_q[slot]
    acts[slot, side, 0] = q.astype(BF16)
    acts[slot, side, 1] = gz
    acts[slot, side, 2] = (z * s).astype(BF16)
    acts[slot, side, 3] = g
    if first:
        return None
    gn = dot_t(gz, weight[0])
    r = save_r[slot][:, :1]
    return (g.astype(F32) + r * (gn - q * jnp.mean(gn * q, axis=-1, keepdims=True))).astype(BF16)


def own_weights_kernel(place, own_a, own_b, half_e, half_d, held_e, held_d, sems):
    rows = pl.ds(pl.multiple_of(place[2] * HALF, HALF), HALF)
    copies = []
    for side, (half, held) in enumerate(((half_e, held_e), (half_d, held_d))):
        for i, own in enumerate((own_a, own_b)):
            copies.append(pltpu.make_async_copy(own.at[side, 0, rows, :], half.at[i], sems.at[len(copies)]))
            copies.append(pltpu.make_async_copy(own.at[side, 0], held.at[place[1], i], sems.at[len(copies)]))
    for copy in copies:
        copy.start()
    for copy in copies:
        copy.wait()


def start_weights(place, pieces, held, sems, order):
    def start(m, apart):
        for part, core in ((pieces[2 * apart - 2], place[2]), (pieces[2 * apart - 1], 1 - place[2])):
            rows = pl.ds(pl.multiple_of(core * HALF, HALF), HALF)
            pltpu.make_async_copy(part, held.at[m, :, rows, :], sems.at[m]).start()

    for m in order:
        for apart in range(1, LEVELS):
            pl.when(place[1] == (m ^ apart))(functools.partial(start, m, apart))


def wait_weights(place, held, sems, m):
    pl.when(place[1] != m)(pltpu.make_async_copy(held.at[m], held.at[m], sems.at[m]).wait)
    return held.at[m]


N_PIECES = 6


UP = tuple(range(LEVELS))
DOWN = tuple(reversed(UP))


def enc_forward_kernel(place, pixels, *refs):
    pieces, (_, hop, e, q, z, r, held, sems) = refs[:N_PIECES], refs[N_PIECES:]
    start_weights(place, pieces, held, sems, UP)

    @pl.when(place[0] == 0)
    def _():
        x = pixels[place[1]]
        for m in UP:
            x = forward_level(x.astype(F32), wait_weights(place, held, sems, m), (q, z, r), m)
            e[m] = x
        hop[...] = x

    @pl.when(place[0] != 0)
    def _():
        for m in UP:
            wait_weights(place, held, sems, m)


def turn_forward_kernel(place, arrived, weights_e, *refs):
    pieces, (_, hop, qe, ze, re, qd, zd, rd, held, sems) = refs[:N_PIECES], refs[N_PIECES:]
    start_weights(place, pieces, held, sems, DOWN)

    @pl.when(place[0] == 1)
    def _():
        x = arrived[...]
        skips = []
        for m in UP:
            x = forward_level(x.astype(F32), weights_e.at[m], (qe, ze, re), m)
            skips.append(x)
        for m in DOWN:
            v = x.astype(F32) + skips[m].astype(F32)
            x = forward_level(v, wait_weights(place, held, sems, m), (qd, zd, rd), m)
        hop[...] = x

    @pl.when(place[0] != 1)
    def _():
        for m in DOWN:
            wait_weights(place, held, sems, m)


def turn_dec_kernel(place, arrived, e, cotangent, weights, hop, skip_grads, acts, q, z, r):
    @pl.when(place[0] == 0)
    def _():
        x = arrived[...]
        for m in DOWN:
            v = x.astype(F32) + e[m].astype(F32)
            x = forward_level(v, weights.at[m], (q, z, r), m)
        g = cotangent[place[1]]
        for m in UP:
            g = backward_level(g, weights.at[m], (q, z, r), m, acts, 1)
            skip_grads[m] = g
        hop[...] = g


def enc_backward(g, skip_grads, weights, save, acts, first=False):
    for m in DOWN:
        g = (g.astype(F32) + skip_grads[m].astype(F32)).astype(BF16)
        g = backward_level(g, weights.at[m], save, m, acts, 0, first and m == 0)
    return g


def turn_backward_kernel(place, arrived, qe, ze, re, qd, zd, rd, weights_e, weights_d, acts_in, hop, acts):
    del acts_in

    @pl.when(place[0] == 1)
    def _():
        g = arrived[...]
        skip_grads = []
        for m in UP:
            g = backward_level(g, weights_d.at[m], (qd, zd, rd), m, acts, 1)
            skip_grads.append(g)
        hop[...] = enc_backward(g, skip_grads, weights_e, (qe, ze, re), acts)


def enc_backward_kernel(place, arrived, q, z, r, skip_grads, weights, acts_in, acts):
    del acts_in

    @pl.when(place[0] == 0)
    def _():
        enc_backward(arrived[...], skip_grads, weights, (q, z, r), acts, first=True)


def grads_kernel(acts, out):
    rows = acts.shape[0] * ROWS
    grad = t_dot(acts[:, 0].reshape(rows, WIDTH), acts[:, 1].reshape(rows, WIDTH))
    for z_low in range(4):
        for z_high in range(4):
            for x in range(2):
                for core in range(2):
                    first = x * 256 + (z_high * 4 + z_low) * 16 + core * 8
                    out[z_low, x, core, z_high] = grad[first : first + 8].astype(BF16)


def last_sum_kernel(factor, parts, grads_a, grads_b):
    total = sum(parts[i].astype(F32) for i in range(4)) * factor
    for side in (0, 1):
        grads_a[side, 0] = total[2 * side]
        grads_b[side, 0] = total[2 * side + 1]


SMEM = pl.BlockSpec(memory_space=pltpu.SMEM)
VMEM = pl.BlockSpec(memory_space=pltpu.VMEM)
ANY = pl.BlockSpec(memory_space=pl.ANY)
PARAMS = pltpu.CompilerParams(vmem_limit_bytes=VMEM_BYTES)

ROW = jax.ShapeDtypeStruct((ROWS, WIDTH), BF16)
STACK = jax.ShapeDtypeStruct((LEVELS, ROWS, WIDTH), BF16)
SAVE = jax.ShapeDtypeStruct((LEVELS, ROWS, WIDTH), F32)
SAVE_R = jax.ShapeDtypeStruct((LEVELS, ROWS, 128), F32)
SAVES = (SAVE, SAVE, SAVE_R)
ACTS = jax.ShapeDtypeStruct((LEVELS, 2, 4, ROWS, WIDTH), BF16)

WEIGHTS = jax.ShapeDtypeStruct((LEVELS, 2, WIDTH, WIDTH), BF16)

SEMS = pltpu.SemaphoreType.DMA((LEVELS,))
SCRATCH_SAVES = tuple(pltpu.VMEM(s.shape, s.dtype) for s in SAVES)


def call(kernel, operands, spaces, outs, out_spaces, scratch=(), aliases=None, name=None):
    return pl.pallas_call(
        kernel,
        out_shape=outs,
        in_specs=spaces,
        out_specs=out_spaces,
        scratch_shapes=scratch,
        input_output_aliases=aliases or {},
        compiler_params=PARAMS,
        name=name,
    )(*operands)


def local(pixels, cotangent, weights_a, weights_b):
    core = lax.axis_index("core")
    level = lax.axis_index(PIPE)
    place = jnp.stack([level // LEVELS, level % LEVELS, core, level]).astype(jnp.int32)

    piece = jax.ShapeDtypeStruct((2, HALF, WIDTH), BF16)
    half_e, half_d, own_e, own_d = call(
        own_weights_kernel, (place, weights_a, weights_b), (SMEM, ANY, ANY), (piece, piece, WEIGHTS, WEIGHTS),
        (VMEM,) * 4, (pltpu.SemaphoreType.DMA((8,)),), name="own_weights",
    )

    def along_x(block):
        return lax.ppermute(block, ("x_lo", "x_hi"), [(i, 3 - i) for i in range(4)])

    def along_y(block):
        return lax.ppermute(block, "y_lo", [(0, 1), (1, 0)])

    def swap(block):
        return lax.ppermute(block, "core", [(0, 1), (1, 0)])

    x_e, y_d = along_x(half_e), along_y(half_d)
    x_d, y_e = along_x(half_d), along_y(half_e)
    diagonal_e, diagonal_d = along_y(x_e), along_x(y_d)

    pieces = []
    for piece in (x_e, y_e, diagonal_e, x_d, y_d):
        pieces += [piece, swap(piece)]
    *pieces, diagonal_d = lax.optimization_barrier((*pieces, diagonal_d))

    up = [(0, 3), (1, 2)]
    down = [(3, 0), (2, 1)]
    y = ("stage", "y_lo")

    hop, e, *saves_0, weights_e = call(
        enc_forward_kernel, (place, pixels, *pieces[:6], own_e), (SMEM, VMEM) + (ANY,) * N_PIECES + (VMEM,),
        (ROW, STACK) + SAVES + (WEIGHTS,), (VMEM,) * 6, (SEMS,), {2 + N_PIECES: 5}, name="enc_forward",
    )
    arrived = lax.ppermute(hop, y, up)
    pieces = (*pieces[6:], diagonal_d, swap(diagonal_d))
    hop, *saves, weights_d = call(
        turn_forward_kernel, (place, arrived, weights_e, *pieces, own_d),
        (SMEM, VMEM, VMEM) + (ANY,) * N_PIECES + (VMEM,),
        (ROW,) + SAVES + SAVES + (WEIGHTS,), (VMEM,) * 8, (SEMS,), {3 + N_PIECES: 7}, name="turn_forward",
    )
    arrived = lax.ppermute(hop, y, down)
    hop, skip_grads, acts = call(
        turn_dec_kernel, (place, arrived, e, cotangent, weights_d), (SMEM,) + (VMEM,) * 4,
        (ROW, STACK, ACTS), (VMEM,) * 3, SCRATCH_SAVES, name="turn_dec",
    )
    arrived = lax.ppermute(hop, y, up)
    hop, acts = call(
        turn_backward_kernel, (place, arrived, *saves, weights_e, weights_d, acts), (SMEM,) + (VMEM,) * 10,
        (ROW, ACTS), (VMEM,) * 2, (), {10: 1}, name="turn_backward",
    )
    arrived = lax.ppermute(hop, y, down)
    acts = call(
        enc_backward_kernel, (place, arrived, *saves_0, skip_grads, weights_e, acts), (SMEM,) + (VMEM,) * 7,
        ACTS, VMEM, (), {7: 0}, name="enc_backward",
    )

    acts = lax.all_to_all(acts.reshape(16, 2, ROWS, WIDTH), MEMBERS + ("x_lo", "core"), 0, 0)
    grad = call(
        grads_kernel, (acts,), (VMEM,), jax.ShapeDtypeStruct((4, 2, 2, 4, 8, WIDTH), BF16), VMEM, name="grads"
    )

    total = lax.all_to_all(grad.reshape(16, 4, 8, WIDTH), ("z_lo", "x_lo", "core"), 0, 0)
    total = jnp.sum(total.astype(F32).reshape(4, 4, 4, 8, WIDTH), axis=0).astype(BF16)
    total = lax.all_to_all(total.transpose(1, 0, 2, 3), "z_hi", 0, 0)
    factor = 1.0 / math.sqrt(LEVELS * ROWS * 64)
    out = jax.ShapeDtypeStruct((2, 1, 8, WIDTH), F32)
    return tuple(
        call(functools.partial(last_sum_kernel, factor), (total,), (VMEM,), (out, out), (VMEM, VMEM), name="last_sum")
    )


MEMBERS = ("y_lo", "x_hi")
DP = ("x_lo", "z_hi", "z_lo", "core")
PIPE = ("stage", "y_lo", "x_hi")


def solution(mesh):
    fine = jax.sharding.Mesh(mesh.devices.reshape(2, 4, 4, 2, 2, 2, 2), DP + PIPE)
    return jax.shard_map(
        local,
        mesh=fine,
        in_specs=(
            P(None, DP, None),
            P(None, DP, None),
            P(None, PIPE, None, None),
            P(None, PIPE, None, None),
        ),
        out_specs=(P(None, PIPE, DP, None), P(None, PIPE, DP, None)),
        check_vma=False,
    )
```

```python
import functools
import math

import jax
import jax.numpy as jnp
from jax import lax
from jax.experimental import pallas as pl
from jax.experimental.pallas import tpu as pltpu
from jax.sharding import PartitionSpec as P

EPS = 1e-06
LEVELS = 4
ROWS = 32
WIDTH = 512
HALF = WIDTH // 2
BF16 = jnp.bfloat16
F32 = jnp.float32
VMEM_BYTES = 26 * 1024 * 1024


def dot(a, b):
    return jnp.dot(a, b, preferred_element_type=F32)


def dot_t(a, b):
    return lax.dot_general(a, b, (((1,), (1,)), ((), ())), preferred_element_type=F32)


def t_dot(a, b):
    return lax.dot_general(a, b, (((0,), (0,)), ((), ())), preferred_element_type=F32)


def forward_level(v, weight, save, slot):
    save_q, save_f, save_h, save_r = save
    r = lax.rsqrt(jnp.mean(v * v, axis=-1, keepdims=True) + EPS)
    q = v * r
    z = dot(q.astype(BF16), weight[0])
    s = jax.nn.sigmoid(z)
    h = (z * s).astype(BF16)
    save_q[slot] = q
    save_f[slot] = s * (1.0 + z * (1.0 - s))
    save_h[slot] = h
    save_r[slot] = jnp.broadcast_to(r, (ROWS, 128))
    return (v + dot(h, weight[1])).astype(BF16)


def backward_level(g, weight, save, slot, acts, side, first=False):
    save_q, save_f, save_h, save_r = save
    gz = (dot_t(g, weight[1]) * save_f[slot]).astype(BF16)
    q = save_q[slot]
    acts[slot, side, 0] = q.astype(BF16)
    acts[slot, side, 1] = gz
    acts[slot, side, 2] = save_h[slot]
    acts[slot, side, 3] = g
    if first:
        return None
    gn = dot_t(gz, weight[0])
    r = save_r[slot][:, :1]
    return (g.astype(F32) + r * (gn - q * jnp.mean(gn * q, axis=-1, keepdims=True))).astype(BF16)


def own_weights_kernel(place, own_a, own_b, half_e, half_d, held_e, held_d, sems):
    rows = pl.ds(pl.multiple_of(place[2] * HALF, HALF), HALF)
    copies = []
    for side, (half, held) in enumerate(((half_e, held_e), (half_d, held_d))):
        for i, own in enumerate((own_a, own_b)):
            copies.append(pltpu.make_async_copy(own.at[side, 0, rows, :], half.at[i], sems.at[len(copies)]))
            copies.append(pltpu.make_async_copy(own.at[side, 0], held.at[place[1], i], sems.at[len(copies)]))
    for copy in copies:
        copy.start()
    for copy in copies:
        copy.wait()


def start_weights(place, pieces, held, sems, order):
    def start(m, apart):
        for part, core in ((pieces[2 * apart - 2], place[2]), (pieces[2 * apart - 1], 1 - place[2])):
            rows = pl.ds(pl.multiple_of(core * HALF, HALF), HALF)
            pltpu.make_async_copy(part, held.at[m, :, rows, :], sems.at[m]).start()

    for m in order:
        for apart in range(1, LEVELS):
            pl.when(place[1] == (m ^ apart))(functools.partial(start, m, apart))


def wait_weights(place, held, sems, m):
    pl.when(place[1] != m)(pltpu.make_async_copy(held.at[m], held.at[m], sems.at[m]).wait)
    return held.at[m]


N_PIECES = 6


UP = tuple(range(LEVELS))
DOWN = tuple(reversed(UP))


def enc_forward_kernel(place, pixels, *refs):
    pieces, (_, hop, e, q, f, h, r, held, sems) = refs[:N_PIECES], refs[N_PIECES:]
    start_weights(place, pieces, held, sems, UP)

    @pl.when(place[0] == 0)
    def _():
        x = pixels[place[1]]
        for m in UP:
            x = forward_level(x.astype(F32), wait_weights(place, held, sems, m), (q, f, h, r), m)
            e[m] = x
        hop[...] = x

    @pl.when(place[0] != 0)
    def _():
        for m in UP:
            wait_weights(place, held, sems, m)


def turn_forward_kernel(place, arrived, weights_e, *refs):
    pieces, (_, hop, qe, fe, he, re, qd, fd, hd, rd, held, sems) = refs[:N_PIECES], refs[N_PIECES:]
    start_weights(place, pieces, held, sems, DOWN)

    @pl.when(place[0] == 1)
    def _():
        x = arrived[...]
        skips = []
        for m in UP:
            x = forward_level(x.astype(F32), weights_e.at[m], (qe, fe, he, re), m)
            skips.append(x)
        for m in DOWN:
            v = x.astype(F32) + skips[m].astype(F32)
            x = forward_level(v, wait_weights(place, held, sems, m), (qd, fd, hd, rd), m)
        hop[...] = x

    @pl.when(place[0] != 1)
    def _():
        for m in DOWN:
            wait_weights(place, held, sems, m)


def turn_dec_kernel(place, arrived, e, cotangent, weights, hop, skip_grads, acts, q, f, h, r):
    @pl.when(place[0] == 0)
    def _():
        x = arrived[...]
        for m in DOWN:
            v = x.astype(F32) + e[m].astype(F32)
            x = forward_level(v, weights.at[m], (q, f, h, r), m)
        g = cotangent[place[1]]
        for m in UP:
            g = backward_level(g, weights.at[m], (q, f, h, r), m, acts, 1)
            skip_grads[m] = g
        hop[...] = g


def enc_backward(g, skip_grads, weights, save, acts, first=False):
    for m in DOWN:
        g = (g.astype(F32) + skip_grads[m].astype(F32)).astype(BF16)
        g = backward_level(g, weights.at[m], save, m, acts, 0, first and m == 0)
    return g


def turn_backward_kernel(place, arrived, qe, fe, he, re, qd, fd, hd, rd, weights_e, weights_d, acts_in, hop, acts):
    del acts_in

    @pl.when(place[0] == 1)
    def _():
        g = arrived[...]
        skip_grads = []
        for m in UP:
            g = backward_level(g, weights_d.at[m], (qd, fd, hd, rd), m, acts, 1)
            skip_grads.append(g)
        hop[...] = enc_backward(g, skip_grads, weights_e, (qe, fe, he, re), acts)


def enc_backward_kernel(place, arrived, q, f, h, r, skip_grads, weights, acts_in, acts):
    del acts_in

    @pl.when(place[0] == 0)
    def _():
        enc_backward(arrived[...], skip_grads, weights, (q, f, h, r), acts, first=True)


def grads_kernel(acts, out):
    rows = acts.shape[0] * ROWS
    grad = t_dot(acts[:, 0].reshape(rows, WIDTH), acts[:, 1].reshape(rows, WIDTH))
    for z_low in range(4):
        for z_high in range(4):
            for x in range(2):
                for core in range(2):
                    first = x * 256 + (z_high * 4 + z_low) * 16 + core * 8
                    out[z_low, x, core, z_high] = grad[first : first + 8].astype(BF16)


def last_sum_kernel(factor, parts, grads_a, grads_b):
    total = sum(parts[i].astype(F32) for i in range(4)) * factor
    for side in (0, 1):
        grads_a[side, 0] = total[2 * side]
        grads_b[side, 0] = total[2 * side + 1]


SMEM = pl.BlockSpec(memory_space=pltpu.SMEM)
VMEM = pl.BlockSpec(memory_space=pltpu.VMEM)
ANY = pl.BlockSpec(memory_space=pl.ANY)
PARAMS = pltpu.CompilerParams(vmem_limit_bytes=VMEM_BYTES)

ROW = jax.ShapeDtypeStruct((ROWS, WIDTH), BF16)
STACK = jax.ShapeDtypeStruct((LEVELS, ROWS, WIDTH), BF16)
SAVE = jax.ShapeDtypeStruct((LEVELS, ROWS, WIDTH), F32)
SAVE_R = jax.ShapeDtypeStruct((LEVELS, ROWS, 128), F32)
SAVES = (SAVE, SAVE, STACK, SAVE_R)
ACTS = jax.ShapeDtypeStruct((LEVELS, 2, 4, ROWS, WIDTH), BF16)

WEIGHTS = jax.ShapeDtypeStruct((LEVELS, 2, WIDTH, WIDTH), BF16)

SEMS = pltpu.SemaphoreType.DMA((LEVELS,))
SCRATCH_SAVES = tuple(pltpu.VMEM(s.shape, s.dtype) for s in SAVES)


def call(kernel, operands, spaces, outs, out_spaces, scratch=(), aliases=None, name=None):
    return pl.pallas_call(
        kernel,
        out_shape=outs,
        in_specs=spaces,
        out_specs=out_spaces,
        scratch_shapes=scratch,
        input_output_aliases=aliases or {},
        compiler_params=PARAMS,
        name=name,
    )(*operands)


def local(pixels, cotangent, weights_a, weights_b):
    core = lax.axis_index("core")
    level = lax.axis_index(PIPE)
    place = jnp.stack([level // LEVELS, level % LEVELS, core, level]).astype(jnp.int32)

    piece = jax.ShapeDtypeStruct((2, HALF, WIDTH), BF16)
    half_e, half_d, own_e, own_d = call(
        own_weights_kernel, (place, weights_a, weights_b), (SMEM, ANY, ANY), (piece, piece, WEIGHTS, WEIGHTS),
        (VMEM,) * 4, (pltpu.SemaphoreType.DMA((8,)),), name="own_weights",
    )

    def along_x(block):
        return lax.ppermute(block, ("x_lo", "x_hi"), [(i, 3 - i) for i in range(4)])

    def along_y(block):
        return lax.ppermute(block, "y_lo", [(0, 1), (1, 0)])

    def swap(block):
        return lax.ppermute(block, "core", [(0, 1), (1, 0)])

    x_e, y_d = along_x(half_e), along_y(half_d)
    x_d, y_e = along_x(half_d), along_y(half_e)
    diagonal_e, diagonal_d = along_y(x_e), along_x(y_d)

    pieces = []
    for piece in (x_e, y_e, diagonal_e, x_d, y_d):
        pieces += [piece, swap(piece)]
    *pieces, diagonal_d = lax.optimization_barrier((*pieces, diagonal_d))

    up = [(0, 3), (1, 2)]
    down = [(3, 0), (2, 1)]
    y = ("stage", "y_lo")

    hop, e, *saves_0, weights_e = call(
        enc_forward_kernel, (place, pixels, *pieces[:6], own_e), (SMEM, VMEM) + (ANY,) * N_PIECES + (VMEM,),
        (ROW, STACK) + SAVES + (WEIGHTS,), (VMEM,) * 7, (SEMS,), {2 + N_PIECES: 6}, name="enc_forward",
    )
    arrived = lax.ppermute(hop, y, up)
    pieces = (*pieces[6:], diagonal_d, swap(diagonal_d))
    hop, *saves, weights_d = call(
        turn_forward_kernel, (place, arrived, weights_e, *pieces, own_d),
        (SMEM, VMEM, VMEM) + (ANY,) * N_PIECES + (VMEM,),
        (ROW,) + SAVES + SAVES + (WEIGHTS,), (VMEM,) * 10, (SEMS,), {3 + N_PIECES: 9}, name="turn_forward",
    )
    arrived = lax.ppermute(hop, y, down)
    hop, skip_grads, acts = call(
        turn_dec_kernel, (place, arrived, e, cotangent, weights_d), (SMEM,) + (VMEM,) * 4,
        (ROW, STACK, ACTS), (VMEM,) * 3, SCRATCH_SAVES, name="turn_dec",
    )
    arrived = lax.ppermute(hop, y, up)
    hop, acts = call(
        turn_backward_kernel, (place, arrived, *saves, weights_e, weights_d, acts), (SMEM,) + (VMEM,) * 12,
        (ROW, ACTS), (VMEM,) * 2, (), {12: 1}, name="turn_backward",
    )
    arrived = lax.ppermute(hop, y, down)
    acts = call(
        enc_backward_kernel, (place, arrived, *saves_0, skip_grads, weights_e, acts), (SMEM,) + (VMEM,) * 8,
        ACTS, VMEM, (), {8: 0}, name="enc_backward",
    )

    acts = lax.all_to_all(acts.reshape(16, 2, ROWS, WIDTH), MEMBERS + ("x_lo", "core"), 0, 0)
    grad = call(
        grads_kernel, (acts,), (VMEM,), jax.ShapeDtypeStruct((4, 2, 2, 4, 8, WIDTH), BF16), VMEM, name="grads"
    )

    total = lax.all_to_all(grad.reshape(16, 4, 8, WIDTH), ("z_lo", "x_lo", "core"), 0, 0)
    total = jnp.sum(total.astype(F32).reshape(4, 4, 4, 8, WIDTH), axis=0).astype(BF16)
    total = lax.all_to_all(total.transpose(1, 0, 2, 3), "z_hi", 0, 0)
    factor = 1.0 / math.sqrt(LEVELS * ROWS * 64)
    out = jax.ShapeDtypeStruct((2, 1, 8, WIDTH), F32)
    return tuple(
        call(functools.partial(last_sum_kernel, factor), (total,), (VMEM,), (out, out), (VMEM, VMEM), name="last_sum")
    )


MEMBERS = ("y_lo", "x_hi")
DP = ("x_lo", "z_hi", "z_lo", "core")
PIPE = ("stage", "y_lo", "x_hi")


def solution(mesh):
    fine = jax.sharding.Mesh(mesh.devices.reshape(2, 4, 4, 2, 2, 2, 2), DP + PIPE)
    return jax.shard_map(
        local,
        mesh=fine,
        in_specs=(
            P(None, DP, None),
            P(None, DP, None),
            P(None, PIPE, None, None),
            P(None, PIPE, None, None),
        ),
        out_specs=(P(None, PIPE, DP, None), P(None, PIPE, DP, None)),
        check_vma=False,
    )
```
